128 devices in a mesh: row: 8 (over z_hi, x), col: 8 (over y, core), rep: 2 (over z_lo).
Axes of the slice: x: 4, y: 4, z: 4 (z_hi: 2, z_lo: 2; z = z_hi * 2 + z_lo), core: 2. Of those that a mesh axis runs over, the one named last changes fastest.
Arguments:
- activations: bfloat16 [2048, 12288], P(('col', 'rep'), 'row'), may hold values from -6 to 6
- out_grad: bfloat16 [2048, 24576], P(('row', 'rep'), 'col'), may hold values from -0.1875 to 0.1875
Outputs:
- weight_grad: bfloat16 [12288, 24576], P('row', 'col')
The draws below stay inside these ranges and needn't reach their ends.
All inputs are finite; a program needn't handle non-finite values.
Results may differ from the reference program's by a relative error of at most 0.0051.
Values may be sent and summed in bfloat16 or wider, within the bound.
No kernel may reach another device: no remote copies, remote signals or barrier semaphores. Data moves between devices by JAX's collectives and lax.ppermute only.
A program may use at most 128 MiB of HBM per device.

```python
import jax
import jax.numpy as jnp
from jax import lax

D = 12288
FF = 24576
TOK_DEV = 128
TOKENS = 2048
N_ROW = 8
N_COL = 8
N_REP = 2


def block_levels(key, extent, cuts, smallest, largest):
    gain = 1.0
    for dim, parts in cuts:
        draws = jax.random.uniform(jax.random.fold_in(jax.random.fold_in(key, 6), dim), (parts,), jnp.float32, smallest / len(cuts), largest / len(cuts))
        gain = gain * jnp.repeat(jnp.exp(draws), extent[dim] // parts).reshape((-1,) + (1,) * (len(extent) - 1 - dim))
    return gain


def gaussian(stream_key, dims, deviation, bound, cuts=(), dtype=jnp.bfloat16):
    result = deviation * jax.random.normal(stream_key, dims, jnp.float32)
    if cuts:
        result = result * block_levels(stream_key, dims, cuts, -0.22, 0.18)
    return jnp.clip(result, -bound, bound).astype(dtype)


def setup_inputs(seed: int = 0) -> dict:
    key_of = jax.random.split(jax.random.key(seed), 3)
    activations = gaussian(key_of[0], (TOKENS, D), 1.0, 6.0, ((0, 16), (1, 8)))
    out_grad = gaussian(key_of[1], (TOKENS, FF), (TOK_DEV * N_COL) ** -0.5, 0.1875, ((0, 16), (1, 8)))
    return {"activations": activations, "out_grad": out_grad}


def reference(activations, out_grad):
    acts = activations.reshape(N_COL, N_REP, TOK_DEV, D)
    grads = out_grad.reshape(N_ROW, N_REP, TOK_DEV, FF)
    total = jnp.zeros((D, FF), jnp.float32)
    for replica in range(N_REP):
        left = acts[:, replica].reshape(N_COL * TOK_DEV, D)
        right = grads[:, replica].reshape(N_ROW * TOK_DEV, FF)
        partial_grad = lax.dot_general(left, right, (((0,), (0,)), ((), ())), preferred_element_type=jnp.float32)
        total = total + partial_grad.astype(jnp.bfloat16).astype(jnp.float32)
    return total.astype(jnp.bfloat16)
```

```python
import functools

import jax
import jax.numpy as jnp
import numpy as np
from jax import lax
from jax.experimental import pallas as pl
from jax.experimental.pallas import tpu as pltpu
from jax.sharding import PartitionSpec as P

AXES = ("row", "col", "rep")
TOK = 128
PAIRS = ((768, 768), (768, 768))
GATHERED = 0


def device(x, y, z, core):
    return ((z // 2) * 4 + x) * 16 + (y * 2 + core) * 2 + z % 2


def every():
    return [(x, y, z, c) for x in range(4) for y in range(4) for z in range(4) for c in range(2)]


def ring(dx, dy, dz):
    pairs = []
    for x, y, z, c in every():
        s = 1 if c == 0 else -1
        to = ((x + s * dx) % 4, (y + s * dy) % 4, (z + s * dz) % 4, c)
        pairs.append((device(x, y, z, c), device(*to)))
    return pairs


X_RING, Y_RING, Z_RING = ring(1, 0, 0), ring(0, 1, 0), ring(0, 0, 1)
CORE_SWAP = [(device(x, y, z, c), device(x, y, z, 1 - c)) for x, y, z, c in every()]
REP_SWAP = [(device(x, y, z, c), device(x, y, z ^ 1, c)) for x, y, z, c in every()]


def tables():
    first = np.zeros((128, 16), np.int32)
    second = np.zeros((128, 16), np.int32)
    plain = np.zeros((128, 16), np.int32)
    for x0, y0, z0, c0 in every():
        me = device(x0, y0, z0, c0)
        s0 = 1 if c0 == 0 else -1

        def place(x, z):
            k = (z // 2) * 4 + x
            y, c = k // 2, k % 2
            s = 1 if c == 0 else -1
            return int(c != c0) * 8 + ((y0 - y) * s) % 4 * 2 + int(z % 2 != z0 % 2)

        for outer in range(4):
            for inner in range(4):
                at = outer * 4 + inner
                first[me, at] = place((x0 - s0 * inner) % 4, (z0 - s0 * outer) % 4)
                second[me, at] = place((x0 - s0 * outer) % 4, (z0 - s0 * inner) % 4)
                plain[me, at] = place(outer, inner)
    return np.stack([first, second, plain], axis=1)


def flip(pieces):
    rows, wide = pieces[0].shape

    def kernel(*refs):
        for n, ref in enumerate(refs[:-1]):
            refs[-1][:, n * rows : (n + 1) * rows] = ref[...].T

    total = rows * len(pieces)
    step = 512
    return pl.pallas_call(
        kernel,
        grid=(wide // step,),
        in_specs=[pl.BlockSpec((rows, step), lambda i: (0, i)) for _ in pieces],
        out_specs=pl.BlockSpec((step, total), lambda i: (i, 0)),
        out_shape=jax.ShapeDtypeStruct((wide, total), jnp.bfloat16),
        compiler_params=pltpu.CompilerParams(vmem_limit_bytes=32 << 20),
        cost_estimate=pl.CostEstimate(flops=0, bytes_accessed=4 * wide * total, transcendentals=0),
    )(*pieces)


def multiply(left, groups, places, before, start, full):
    widths = [g[0].shape[1] for g, _ in groups]
    width = sum(widths)
    rows = left[0].shape[0]
    step = 256
    counts = [len(g) for g, _ in groups]
    tokens = sum(a.shape[1] for a in left)

    def kernel(places_ref, *refs):
        left_refs = refs[: len(left)]
        refs = refs[len(left) :]
        grad_refs = refs[: sum(counts)]
        out_ref, held = refs[-2], refs[-1]

        @pl.when(pl.program_id(0) == 0)
        def _():
            n, column = 0, 0
            for (g, row), w in zip(groups, widths):
                at = 0
                for block in g:
                    for piece in range(block.shape[0] // TOK):
                        to = pl.multiple_of(places_ref[row, at] * TOK, TOK)
                        held[pl.ds(to, TOK), column : column + w] = grad_refs[n][
                            piece * TOK : (piece + 1) * TOK, :
                        ]
                        at += 1
                    n += 1
                column += w

        lhs = jnp.concatenate([r[...] for r in left_refs], axis=1) if len(left) > 1 else left_refs[0][...]
        out_ref[...] = jnp.dot(lhs, held[...], preferred_element_type=jnp.float32).astype(jnp.bfloat16)

    operands = list(left) + [b for g, _ in groups for b in g]
    in_specs = [pl.BlockSpec((step, a.shape[1]), lambda i, t: (i, 0)) for a in left]
    in_specs += [
        pl.BlockSpec(b.shape, lambda i, t: (0, 0), pipeline_mode=pl.Buffered(1)) for g, _ in groups for b in g
    ]
    aliases = {}
    if before is not None:
        operands.append(before)
        in_specs.append(pl.BlockSpec(memory_space=pl.ANY))
        aliases = {len(operands): 0}
    assert start % width == 0
    column_block = start // width
    return pl.pallas_call(
        kernel,
        grid_spec=pltpu.PrefetchScalarGridSpec(
            num_scalar_prefetch=1,
            grid=(rows // step,),
            in_specs=in_specs,
            out_specs=pl.BlockSpec((step, width), lambda i, t: (i, column_block)),
            scratch_shapes=[pltpu.VMEM((tokens, width), jnp.bfloat16)],
        ),
        out_shape=jax.ShapeDtypeStruct((rows, full), jnp.bfloat16),
        input_output_aliases=aliases,
        compiler_params=pltpu.CompilerParams(vmem_limit_bytes=32 << 20),
        cost_estimate=pl.CostEstimate(
            flops=2 * rows * width * tokens,
            bytes_accessed=2 * (rows * tokens + tokens * width + rows * width),
            transcendentals=0,
        ),
    )(places, *operands)


def around(block, pairs):
    blocks = [block]
    for _ in range(3):
        blocks.append(lax.ppermute(blocks[-1], AXES, pairs))
    return blocks


def shards(activations, out_grad):
    full = out_grad.shape[1]
    me = (lax.axis_index("row") * 8 + lax.axis_index("col")) * 2 + lax.axis_index("rep")
    places = lax.dynamic_index_in_dim(jnp.asarray(tables()), me, 0, keepdims=False)

    other = lax.ppermute(activations, AXES, REP_SWAP)
    mine = around(jnp.concatenate([activations, other], axis=0), Y_RING)
    sibling = [lax.ppermute(b, AXES, CORE_SWAP) for b in mine]
    left = [flip(mine), flip(sibling)]

    result = None
    start = 0
    jobs = []
    for w_a, w_b in PAIRS:
        a = out_grad[:, start : start + w_a]
        b = out_grad[:, start + w_a : start + w_a + w_b]
        a = around(jnp.concatenate(around(a, X_RING), axis=0), Z_RING)
        b = around(jnp.concatenate(around(b, Z_RING), axis=0), X_RING)
        jobs.append(([(a, 0), (b, 1)], start))
        start += w_a + w_b
    if GATHERED:
        order = [[((z // 2) * 4 + x) * 2 + z % 2 for x in range(4) for z in range(4)]]
        whole = lax.all_gather(
            out_grad[:, start:], ("row", "rep"), axis=0, tiled=True, axis_index_groups=order
        )
        jobs.append(([([whole], 2)], start))
    for groups, at in jobs:
        result = multiply(left, groups, places, result, at, full)
    return result


def solution(mesh):
    placed = (P(("col", "rep"), "row"), P(("row", "rep"), "col"))
    return jax.shard_map(
        shards, mesh=mesh, in_specs=placed, out_specs=P("row", "col"), check_vma=False
    )
```

```python
import jax
import jax.numpy as jnp
import numpy as np
from jax import lax
from jax.experimental import pallas as pl
from jax.experimental.pallas import tpu as pltpu
from jax.sharding import PartitionSpec as P

AXES = ("row", "col", "rep")
TOK = 128
LIMIT = 16
TIES = 2
EARLY = 1
LEFT = 1
F32 = jnp.float32
BF16 = jnp.bfloat16


def device(x, y, z, core):
    return ((z // 2) * 4 + x) * 16 + (y * 2 + core) * 2 + z % 2


def every():
    return [(x, y, z, c) for x in range(4) for y in range(4) for z in range(4) for c in range(2)]


def ring(dx, dy, dz):
    pairs = []
    for x, y, z, c in every():
        s = 1 if c == 0 else -1
        to = ((x + s * dx) % 4, (y + s * dy) % 4, (z + s * dz) % 4, c)
        pairs.append((device(x, y, z, c), device(*to)))
    return pairs


X_RING, Z_RING = ring(1, 0, 0), ring(0, 0, 1)
Y_RING, Y_BACK = ring(0, 1, 0), ring(0, -1, 0)
CORE_SWAP = [(device(x, y, z, c), device(x, y, z, 1 - c)) for x, y, z, c in every()]
REP_SWAP = [(device(x, y, z, c), device(x, y, z ^ 1, c)) for x, y, z, c in every()]

KINDS = [[(i, j) for j in (p, p + 2) for i in range(4)] for p in range(2)]


def inner(part, step):
    return [(i, step) if part == 0 else (step, i) for i in (1, 2, 3)]


PASSES = [
    [[(0, 0), (1, 0), (2, 0), (0, 2)] for p in range(2)],
    [[(3, 0), (0, 1), (0, 3)] + inner(p, 1) for p in range(2)],
    [inner(p, 2) + inner(p, 3) for p in range(2)],
]


def tables():
    out = np.zeros((128, 2, 8), np.int32)
    for x0, y0, z0, c0 in every():
        s0 = 1 if c0 == 0 else -1
        for kind in range(2):
            for at, (i, j) in enumerate(KINDS[kind]):
                x, z = (x0 - s0 * i) % 4, (z0 - s0 * j) % 4
                assert z % 2 == (z0 + kind) % 2
                k = (z // 2) * 4 + x
                y, c = k // 2, k % 2
                s = 1 if c == 0 else -1
                back = ((y0 - y) * s) % 4
                out[device(x0, y0, z0, c0), kind, int(c != c0) * 4 + (0, 1, 3, 2)[back]] = at
    return out


def sort_tokens(places, kind, pieces):
    arrays = [p[0] for p in pieces]
    wide = arrays[0].shape[1]
    step = 512

    def kernel(places_ref, *refs):
        n = 0
        for ref, (_, first, blocks) in zip(refs, pieces):
            for b in range(blocks):
                to = pl.multiple_of(places_ref[kind, n] * TOK, TOK)
                refs[-1][pl.ds(to, TOK), :] = ref[first + b * TOK : first + (b + 1) * TOK, :]
                n += 1

    total = TOK * 8
    return pl.pallas_call(
        kernel,
        grid_spec=pltpu.PrefetchScalarGridSpec(
            num_scalar_prefetch=1,
            grid=(wide // step,),
            in_specs=[pl.BlockSpec((a.shape[0], step), lambda i, t: (0, i)) for a in arrays],
            out_specs=pl.BlockSpec((total, step), lambda i, t: (0, i)),
        ),
        out_shape=jax.ShapeDtypeStruct((total, wide), BF16),
        compiler_params=pltpu.CompilerParams(vmem_limit_bytes=LIMIT << 20),
        cost_estimate=pl.CostEstimate(flops=0, bytes_accessed=4 * wide * total, transcendentals=0),
    )(places, *arrays)


def multiply(lefts, number, shared, own, group, partial, before, full):
    width = full // 4
    used = [l for l in lefts if l is not None]
    slot = [None if l is None else sum(m is not None for m in lefts[:n]) for n, l in enumerate(lefts)]
    rows = used[0].shape[1]
    step = 256
    order = PASSES[number]
    depth = TOK * len(order[0])
    n_own = len(own[0])

    def kernel(*refs):
        left_refs, refs = refs[: len(used)], refs[len(used) :]
        shared_refs, refs = refs[: len(shared)], refs[len(shared) :]
        own_refs = [refs[:n_own], refs[n_own : 2 * n_own]]
        refs = refs[2 * n_own :]
        out_ref = refs[-1]
        for part in range(2):
            cols = slice(part * width, (part + 1) * width)
            lhs = []
            for i, j in order[part]:
                at = KINDS[j % 2].index((i, j)) * TOK
                lhs.append(left_refs[slot[j % 2]][at : at + TOK, :])
            lhs = jnp.concatenate(lhs, axis=0)
            rhs = [r[:, cols] for r in shared_refs] + [r[...] for r in own_refs[part]]
            rhs = jnp.concatenate(rhs, axis=0)
            total = lax.dot_general(lhs, rhs, (((0,), (0,)), ((), ())), preferred_element_type=F32)
            if partial is not None:
                total = total + refs[0][:, cols]
            out_ref[:, cols] = total.astype(out_ref.dtype)

    once = pl.Buffered(1)
    operands = used + list(shared) + list(own[0]) + list(own[1])
    high = TOK * 8
    in_specs = [pl.BlockSpec((high, step), lambda m: (0, m)) for _ in used]
    in_specs += [pl.BlockSpec((TOK, 2 * width), lambda m: (0, group), pipeline_mode=once) for _ in shared]
    in_specs += [pl.BlockSpec(b.shape, lambda m: (0, 0), pipeline_mode=once) for b in own[0] + own[1]]
    aliases = {}
    if partial is not None:
        if number < 2:
            aliases = {len(operands): 0}
        operands.append(partial)
        in_specs.append(pl.BlockSpec((step, 2 * width), lambda m: (m, 0)))
    if number == 2:
        out_specs = pl.BlockSpec((step, 2 * width), lambda m: (m, group))
        out_shape = jax.ShapeDtypeStruct((rows, full), BF16)
        if before is not None:
            aliases = {len(operands): 0}
            operands.append(before)
            in_specs.append(pl.BlockSpec(memory_space=pl.ANY))
    else:
        out_specs = pl.BlockSpec((step, 2 * width), lambda m: (m, 0))
        out_shape = jax.ShapeDtypeStruct((rows, 2 * width), F32)
    return pl.pallas_call(
        kernel,
        grid=(rows // step,),
        in_specs=in_specs,
        out_specs=out_specs,
        out_shape=out_shape,
        input_output_aliases=aliases,
        compiler_params=pltpu.CompilerParams(vmem_limit_bytes=LIMIT << 20),
        cost_estimate=pl.CostEstimate(
            flops=4 * rows * width * depth,
            bytes_accessed=4 * rows * TOK * 8 + 4 * depth * width + 12 * rows * width,
            transcendentals=0,
        ),
    )(*operands)


def send(block, pairs):
    return lax.ppermute(block, AXES, pairs)


def join(blocks, cols=slice(None)):
    return jnp.concatenate([b[:, cols] for b in blocks], axis=0)


def shards(activations, out_grad):
    full = out_grad.shape[1]
    width = full // 4
    me = (lax.axis_index("row") * 8 + lax.axis_index("col")) * 2 + lax.axis_index("rep")
    places = lax.dynamic_index_in_dim(jnp.asarray(tables()), me, 0, keepdims=False)
    tie = lax.optimization_barrier

    x1, z1 = send(out_grad, X_RING), send(out_grad, Z_RING)
    other = send(activations, REP_SWAP)
    up, down = send(activations, Y_RING), send(activations, Y_BACK)
    x1, z1, other, up, down = tie((x1, z1, other, up, down))

    x2, z2 = send(x1, X_RING), send(z1, Z_RING)
    far = send(up, Y_RING)
    other_up = send(other, Y_RING)
    swap_1 = send(join([activations, up, down]), CORE_SWAP)
    x2, z2, far, other_up, swap_1 = tie((x2, z2, far, other_up, swap_1))

    x3, z3 = send(x2, X_RING), send(z2, Z_RING)
    other_far, other_down = send(other_up, Y_RING), send(other, Y_BACK)
    swap_2 = send(join([far, other, other_up]), CORE_SWAP)
    mine = [(b, 0, 1) for b in (activations, up, down, far)]
    left_own = sort_tokens(places, 0, mine + [(swap_1, 0, 3), (swap_2, 0, 1)])
    first = [out_grad, x1, x2, z2]
    sums = [multiply([left_own, None], 0, first, [[], []], g, None, None, full) for g in range(2)]
    if EARLY == 0:
        x3, z3, other_far, other_down, swap_2, left_own = tie((x3, z3, other_far, other_down, swap_2, left_own))
    if EARLY == 1:
        x3, z3, other_far, other_down, swap_2, sums[0] = tie((x3, z3, other_far, other_down, swap_2, sums[0]))
    if EARLY == 2:
        x3, z3, other_far, other_down, swap_2, sums = tie((x3, z3, other_far, other_down, swap_2, sums))

    swap_3 = send(join([other_down, other_far]), CORE_SWAP)
    others = [(b, 0, 1) for b in (other, other_up, other_down, other_far)]
    left_other = sort_tokens(places, 1, others + [(swap_2, TOK, 2), (swap_3, 0, 2)])

    a, b = [[], []], [[], []]
    for g in range(2):
        at = 2 * g * width
        a[g].append(send(join([x1, x2, x3], slice(at, at + width)), Z_RING))
        b[g].append(send(join([z1, z2, z3], slice(at + width, at + 2 * width)), X_RING))
    if TIES >= 1:
        a[0][0], b[0][0], sums[0], sums[1] = tie((a[0][0], b[0][0], sums[0], sums[1]))
    if LEFT:
        a[1][0], b[1][0], left_other = tie((a[1][0], b[1][0], left_other))
    lefts = [left_own, left_other]
    for g in range(2):
        sums[g] = multiply(lefts, 1, [x3, z1, z3], (a[g][:1], b[g][:1]), g, sums[g], None, full)
    for step in range(2):
        for g in range(2):
            if step == 1 and TIES >= 2 + g:
                a[g][1], b[g][1], sums[g] = tie((a[g][1], b[g][1], sums[g]))
            a[g].append(send(a[g][-1], Z_RING))
            b[g].append(send(b[g][-1], X_RING))
    result = None
    for g in range(2):
        result = multiply(lefts, 2, [], (a[g][1:], b[g][1:]), g, sums[g], result, full)
    return result


def solution(mesh):
    placed = (P(("col", "rep"), "row"), P(("row", "rep"), "col"))
    return jax.shard_map(
        shards, mesh=mesh, in_specs=placed, out_specs=P("row", "col"), check_vma=False
    )
```

```python
import jax
import jax.numpy as jnp
import numpy as np
from jax import lax
from jax.experimental import pallas as pl
from jax.experimental.pallas import tpu as pltpu
from jax.sharding import PartitionSpec as P

AXES = ("row", "col", "rep")
TOK = 128
LIMIT = 16
TIES = 2
HOLD = 2
SPLIT = 1
SWAP = 0
STEP = 512
F32 = jnp.float32
BF16 = jnp.bfloat16


def device(x, y, z, core):
    return ((z // 2) * 4 + x) * 16 + (y * 2 + core) * 2 + z % 2


def every():
    return [(x, y, z, c) for x in range(4) for y in range(4) for z in range(4) for c in range(2)]


def ring(dx, dy, dz):
    pairs = []
    for x, y, z, c in every():
        s = 1 if c == 0 else -1
        to = ((x + s * dx) % 4, (y + s * dy) % 4, (z + s * dz) % 4, c)
        pairs.append((device(x, y, z, c), device(*to)))
    return pairs


X_RING, Z_RING = ring(1, 0, 0), ring(0, 0, 1)
Y_RING, Y_BACK = ring(0, 1, 0), ring(0, -1, 0)
CORE_SWAP = [(device(x, y, z, c), device(x, y, z, 1 - c)) for x, y, z, c in every()]
REP_SWAP = [(device(x, y, z, c), device(x, y, z ^ 1, c)) for x, y, z, c in every()]

KINDS = [
    [(0, 0), (1, 0), (2, 0), (0, 2), (3, 0), (1, 2), (2, 2), (3, 2)],
    [(i, j) for j in (1, 3) for i in range(4)],
]


def inner(part, step):
    return [(i, step) if part == 0 else (step, i) for i in (1, 2, 3)]


PASSES = [
    [[(0, 0), (1, 0), (2, 0), (0, 2)] for p in range(2)],
    [[(3, 0), (0, 1), (0, 3)] + inner(p, 1) for p in range(2)],
    [inner(p, 2) + inner(p, 3) for p in range(2)],
]


def tables():
    out = np.zeros((128, 2, 8), np.int32)
    for x0, y0, z0, c0 in every():
        s0 = 1 if c0 == 0 else -1
        for kind in range(2):
            for at, (i, j) in enumerate(KINDS[kind]):
                x, z = (x0 - s0 * i) % 4, (z0 - s0 * j) % 4
                assert z % 2 == (z0 + kind) % 2
                k = (z // 2) * 4 + x
                y, c = k // 2, k % 2
                s = 1 if c == 0 else -1
                back = ((y0 - y) * s) % 4
                out[device(x0, y0, z0, c0), kind, int(c != c0) * 4 + (0, 1, 3, 2)[back]] = at
    return out


def sort_tokens(places, kind, pieces):
    arrays = [p[0] for p in pieces]
    wide = arrays[0].shape[1]

    def kernel(places_ref, *refs):
        sems = refs[-1]
        copies = []
        for ref, (_, first, blocks) in zip(refs, pieces):
            for b in range(blocks):
                n = len(copies)
                to = pl.multiple_of(places_ref[kind, n] * TOK, TOK)
                copies.append(
                    pltpu.make_async_copy(
                        ref.at[pl.ds(first + b * TOK, TOK)], refs[-2].at[pl.ds(to, TOK)], sems.at[n]
                    )
                )
                copies[-1].start()
        for copy in copies:
            copy.wait()

    total = TOK * 8
    return pl.pallas_call(
        kernel,
        grid_spec=pltpu.PrefetchScalarGridSpec(
            num_scalar_prefetch=1,
            grid=(1,),
            in_specs=[pl.BlockSpec(memory_space=pl.ANY) for a in arrays],
            out_specs=pl.BlockSpec(memory_space=pl.ANY),
            scratch_shapes=[pltpu.SemaphoreType.DMA((8,))],
        ),
        out_shape=jax.ShapeDtypeStruct((total, wide), BF16),
        compiler_params=pltpu.CompilerParams(vmem_limit_bytes=1 << 20),
        cost_estimate=pl.CostEstimate(flops=0, bytes_accessed=4 * wide * total, transcendentals=0),
    )(places, *arrays)


def multiply(lefts, number, shared, own, group, partial, before, full):
    width = full // 4
    used = [l for l in lefts if l is not None]
    slot = [None if l is None else sum(m is not None for m in lefts[:n]) for n, l in enumerate(lefts)]
    rows = used[0].shape[1]
    step = STEP
    order = PASSES[number]
    depth = TOK * len(order[0])
    n_own = len(own[0])
    skip = (0 if number == 0 else 4, 0)

    def kernel(*refs):
        left_refs, refs = refs[: len(used)], refs[len(used) :]
        shared_refs, refs = refs[: len(shared)], refs[len(shared) :]
        own_refs = [refs[:n_own], refs[n_own : 2 * n_own]]
        refs = refs[2 * n_own :]
        out_ref = refs[-1]
        for part in range(2):
            cols = slice(part * width, (part + 1) * width)
            lhs = []
            for i, j in order[part]:
                at = (KINDS[j % 2].index((i, j)) - skip[j % 2]) * TOK
                lhs.append(left_refs[slot[j % 2]][at : at + TOK, :])
            lhs = jnp.concatenate(lhs, axis=0)
            rhs = [r[:, cols] for r in shared_refs] + [r[...] for r in own_refs[part]]
            rhs = jnp.concatenate(rhs, axis=0)
            total = lax.dot_general(lhs, rhs, (((0,), (0,)), ((), ())), preferred_element_type=F32)
            if partial is not None:
                total = total + refs[0][:, cols]
            out_ref[:, cols] = total.astype(out_ref.dtype)

    once = pl.Buffered(1)
    operands = used + list(shared) + list(own[0]) + list(own[1])
    in_specs = [pl.BlockSpec((4 * TOK, step), lambda m: (skip[0] // 4, m))]
    in_specs += [pl.BlockSpec((8 * TOK, step), lambda m: (0, m)) for _ in used[1:]]
    in_specs += [pl.BlockSpec((TOK, 2 * width), lambda m: (0, group), pipeline_mode=once) for _ in shared]
    in_specs += [pl.BlockSpec(b.shape, lambda m: (0, 0), pipeline_mode=once) for b in own[0] + own[1]]
    aliases = {}
    if partial is not None:
        if number < 2:
            aliases = {len(operands): 0}
        operands.append(partial)
        in_specs.append(pl.BlockSpec((step, 2 * width), lambda m: (m, 0)))
    if number == 2:
        out_specs = pl.BlockSpec((step, 2 * width), lambda m: (m, group))
        out_shape = jax.ShapeDtypeStruct((rows, full), BF16)
        if before is not None:
            aliases = {len(operands): 0}
            operands.append(before)
            in_specs.append(pl.BlockSpec(memory_space=pl.ANY))
    else:
        out_specs = pl.BlockSpec((step, 2 * width), lambda m: (m, 0))
        out_shape = jax.ShapeDtypeStruct((rows, 2 * width), F32)
    return pl.pallas_call(
        kernel,
        grid=(rows // step,),
        in_specs=in_specs,
        out_specs=out_specs,
        out_shape=out_shape,
        input_output_aliases=aliases,
        compiler_params=pltpu.CompilerParams(vmem_limit_bytes=LIMIT << 20),
        cost_estimate=pl.CostEstimate(
            flops=4 * rows * width * depth,
            bytes_accessed=4 * rows * TOK * 8 + 4 * depth * width + 12 * rows * width,
            transcendentals=0,
        ),
    )(*operands)


def send(block, pairs):
    return lax.ppermute(block, AXES, pairs)


def join(blocks, cols=slice(None)):
    return jnp.concatenate([b[:, cols] for b in blocks], axis=0)


def whole(arrays):
    return [(a, 0, a.shape[0] // TOK) for a in arrays]


def shards(activations, out_grad):
    full = out_grad.shape[1]
    width = full // 4
    me = (lax.axis_index("row") * 8 + lax.axis_index("col")) * 2 + lax.axis_index("rep")
    places = lax.dynamic_index_in_dim(jnp.asarray(tables()), me, 0, keepdims=False)
    tie = lax.optimization_barrier

    x1, z1 = send(out_grad, X_RING), send(out_grad, Z_RING)
    other = send(activations, REP_SWAP)
    up, down = send(activations, Y_RING), send(activations, Y_BACK)
    x1, z1, other, up, down = tie((x1, z1, other, up, down))

    x2, z2 = send(x1, X_RING), send(z1, Z_RING)
    far = send(up, Y_RING)
    other_up = send(other, Y_RING)
    if SWAP == 0:
        swap_1 = [send(join([activations, up, down]), CORE_SWAP)]
    else:
        swap_1 = []
    x2, z2 = tie((x2, z2))
    x3, z3 = send(x2, X_RING), send(z2, Z_RING)
    if HOLD:
        x2, z2, far, other, other_up, swap_1 = tie((x2, z2, far, other, other_up, swap_1))
    else:
        far, other, other_up, swap_1 = tie((far, other, other_up, swap_1))

    other_far, other_down = send(other_up, Y_RING), send(other, Y_BACK)
    if SWAP == 0:
        swap_2 = [send(far, CORE_SWAP)]
    elif SWAP == 1:
        swap_2 = [send(join([activations, up, down, far]), CORE_SWAP)]
    else:
        swap_2 = [send(t, CORE_SWAP) for t in (activations, up, down, far)]
    owns = len(swap_2)
    swap_2.append(send(join([other, other_up]), CORE_SWAP))
    mine = whole([activations, up, down, far])
    left_own = sort_tokens(places, 0, mine + whole(swap_1 + swap_2[:owns]))
    if HOLD > 1:
        left_own, x3, z3 = tie((left_own, x3, z3))
    first = [out_grad, x1, x2, z2]
    sums = [multiply([left_own, None], 0, first, [[], []], g, None, None, full) for g in range(2)]
    other_far, other_down, swap_2 = tie((other_far, other_down, swap_2))

    swap_3 = [send(join([other_down, other_far]), CORE_SWAP)]
    others = whole([other, other_up, other_down, other_far])
    left_other = sort_tokens(places, 1, others + whole(swap_2[owns:] + swap_3))

    a, b = [[], []], [[], []]
    for g in range(2):
        at = 2 * g * width
        a[g].append(send(join([x1, x2, x3], slice(at, at + width)), Z_RING))
        b[g].append(send(join([z1, z2, z3], slice(at + width, at + 2 * width)), X_RING))
    if SPLIT:
        a[0][0], b[0][0], sums[0] = tie((a[0][0], b[0][0], sums[0]))
        a[1][0], b[1][0], left_other, sums[1] = tie((a[1][0], b[1][0], left_other, sums[1]))
    else:
        a[0][0], b[0][0], sums[0], sums[1] = tie((a[0][0], b[0][0], sums[0], sums[1]))
        a[1][0], b[1][0], left_other = tie((a[1][0], b[1][0], left_other))
    lefts = [left_own, left_other]
    for g in range(2):
        sums[g] = multiply(lefts, 1, [x3, z1, z3], (a[g][:1], b[g][:1]), g, sums[g], None, full)
    for step in range(2):
        for g in range(2):
            if step == 1 and TIES >= 2 + g:
                a[g][1], b[g][1], sums[g] = tie((a[g][1], b[g][1], sums[g]))
            a[g].append(send(a[g][-1], Z_RING))
            b[g].append(send(b[g][-1], X_RING))
    result = None
    for g in range(2):
        result = multiply(lefts, 2, [], (a[g][1:], b[g][1:]), g, sums[g], result, full)
    return result


def solution(mesh):
    placed = (P(("col", "rep"), "row"), P(("row", "rep"), "col"))
    return jax.shard_map(
        shards, mesh=mesh, in_specs=placed, out_specs=P("row", "col"), check_vma=False
    )
```

```python
import jax
import jax.numpy as jnp
import numpy as np
from jax import lax
from jax.experimental import pallas as pl
from jax.experimental.pallas import tpu as pltpu
from jax.sharding import PartitionSpec as P

AXES = ("row", "col", "rep")
TOK = 128
LIMIT = 19
STEP = 512
F32 = jnp.float32
BF16 = jnp.bfloat16


def device(x, y, z, core):
    return ((z // 2) * 4 + x) * 16 + (y * 2 + core) * 2 + z % 2


def every():
    return [(x, y, z, c) for x in range(4) for y in range(4) for z in range(4) for c in range(2)]


def ring(dx, dy, dz):
    pairs = []
    for x, y, z, c in every():
        s = 1 if c == 0 else -1
        to = ((x + s * dx) % 4, (y + s * dy) % 4, (z + s * dz) % 4, c)
        pairs.append((device(x, y, z, c), device(*to)))
    return pairs


X_RING, Z_RING = ring(1, 0, 0), ring(0, 0, 1)
Y_RING, Y_BACK = ring(0, 1, 0), ring(0, -1, 0)
CORE_SWAP = [(device(x, y, z, c), device(x, y, z, 1 - c)) for x, y, z, c in every()]
REP_SWAP = [(device(x, y, z, c), device(x, y, z ^ 1, c)) for x, y, z, c in every()]

KINDS = [
    [(0, 0), (1, 0), (2, 0), (0, 2), (3, 0), (1, 2), (2, 2), (3, 2)],
    [(i, j) for j in (1, 3) for i in range(4)],
]


def inner(part, step):
    return [(i, step) if part == 0 else (step, i) for i in (1, 2, 3)]


PASSES = [
    [[(0, 0), (1, 0), (2, 0), (0, 2)] for p in range(2)],
    [[(3, 0), (0, 1), (0, 3)] + inner(p, 1) for p in range(2)],
    [inner(p, 2) + inner(p, 3) for p in range(2)],
]


def tables():
    out = np.zeros((128, 2, 8), np.int32)
    for x0, y0, z0, c0 in every():
        s0 = 1 if c0 == 0 else -1
        for kind in range(2):
            for at, (i, j) in enumerate(KINDS[kind]):
                x, z = (x0 - s0 * i) % 4, (z0 - s0 * j) % 4
                assert z % 2 == (z0 + kind) % 2
                k = (z // 2) * 4 + x
                y, c = k // 2, k % 2
                s = 1 if c == 0 else -1
                back = ((y0 - y) * s) % 4
                out[device(x0, y0, z0, c0), kind, int(c != c0) * 4 + (0, 1, 3, 2)[back]] = at
    return out


def sort_tokens(places, kind, pieces):
    arrays = [p[0] for p in pieces]
    wide = arrays[0].shape[1]

    def kernel(places_ref, *refs):
        sems = refs[-1]
        copies = []
        for ref, (_, first, blocks) in zip(refs, pieces):
            for b in range(blocks):
                n = len(copies)
                to = pl.multiple_of(places_ref[kind, n] * TOK, TOK)
                copies.append(
                    pltpu.make_async_copy(
                        ref.at[pl.ds(first + b * TOK, TOK)], refs[-2].at[pl.ds(to, TOK)], sems.at[n]
                    )
                )
                copies[-1].start()
        for copy in copies:
            copy.wait()

    total = TOK * 8
    return pl.pallas_call(
        kernel,
        grid_spec=pltpu.PrefetchScalarGridSpec(
            num_scalar_prefetch=1,
            grid=(1,),
            in_specs=[pl.BlockSpec(memory_space=pl.ANY) for a in arrays],
            out_specs=pl.BlockSpec(memory_space=pl.ANY),
            scratch_shapes=[pltpu.SemaphoreType.DMA((8,))],
        ),
        out_shape=jax.ShapeDtypeStruct((total, wide), BF16),
        compiler_params=pltpu.CompilerParams(vmem_limit_bytes=1 << 20),
        cost_estimate=pl.CostEstimate(flops=0, bytes_accessed=4 * wide * total, transcendentals=0),
    )(places, *arrays)


def multiply(lefts, number, shared, own, group, partial, before, full):
    width = full // 4
    used = [l for l in lefts if l is not None]
    slot = [None if l is None else sum(m is not None for m in lefts[:n]) for n, l in enumerate(lefts)]
    rows = used[0].shape[1]
    step = STEP
    order = PASSES[number]
    depth = TOK * len(order[0])
    n_own = len(own[0])
    skip = (4 if number in (1, 2) else 0, 0)

    def kernel(*refs):
        left_refs, refs = refs[: len(used)], refs[len(used) :]
        shared_refs, refs = refs[: len(shared)], refs[len(shared) :]
        own_refs = [refs[:n_own], refs[n_own : 2 * n_own]]
        refs = refs[2 * n_own :]
        out_ref = refs[-1]
        for part in range(2):
            cols = slice(part * width, (part + 1) * width)
            lhs = []
            for i, j in order[part]:
                at = (KINDS[j % 2].index((i, j)) - skip[j % 2]) * TOK
                lhs.append(left_refs[slot[j % 2]][at : at + TOK, :])
            lhs = jnp.concatenate(lhs, axis=0)
            rhs = [r[:, cols] for r in shared_refs] + [r[...] for r in own_refs[part]]
            rhs = jnp.concatenate(rhs, axis=0)
            total = lax.dot_general(lhs, rhs, (((0,), (0,)), ((), ())), preferred_element_type=F32)
            if partial is not None:
                total = total + refs[0][:, cols]
            out_ref[:, cols] = total.astype(out_ref.dtype)

    once = pl.Buffered(1)
    operands = used + list(shared) + list(own[0]) + list(own[1])
    in_specs = [pl.BlockSpec((4 * TOK, step), lambda m: (skip[0] // 4, m))]
    in_specs += [pl.BlockSpec((8 * TOK, step), lambda m: (0, m)) for _ in used[1:]]
    in_specs += [pl.BlockSpec((TOK, 2 * width), lambda m: (0, group), pipeline_mode=once) for _ in shared]
    in_specs += [pl.BlockSpec(b.shape, lambda m: (0, 0), pipeline_mode=once) for b in own[0] + own[1]]
    aliases = {}
    if partial is not None:
        if number < 2:
            aliases = {len(operands): 0}
        operands.append(partial)
        in_specs.append(pl.BlockSpec((step, 2 * width), lambda m: (m, 0)))
    if number == 2:
        out_specs = pl.BlockSpec((step, 2 * width), lambda m: (m, group))
        out_shape = jax.ShapeDtypeStruct((rows, full), BF16)
        if before is not None:
            aliases = {len(operands): 0}
            operands.append(before)
            in_specs.append(pl.BlockSpec(memory_space=pl.ANY))
    else:
        out_specs = pl.BlockSpec((step, 2 * width), lambda m: (m, 0))
        out_shape = jax.ShapeDtypeStruct((rows, 2 * width), F32)
    return pl.pallas_call(
        kernel,
        grid=(rows // step,),
        in_specs=in_specs,
        out_specs=out_specs,
        out_shape=out_shape,
        input_output_aliases=aliases,
        compiler_params=pltpu.CompilerParams(vmem_limit_bytes=LIMIT << 20),
        cost_estimate=pl.CostEstimate(
            flops=4 * rows * width * depth,
            bytes_accessed=4 * rows * TOK * 8 + 4 * depth * width + 12 * rows * width,
            transcendentals=0,
        ),
    )(*operands)


def send(block, pairs):
    return lax.ppermute(block, AXES, pairs)


def join(blocks, cols=slice(None)):
    return jnp.concatenate([b[:, cols] for b in blocks], axis=0)


def whole(arrays):
    return [(a, 0, a.shape[0] // TOK) for a in arrays]


def shards(activations, out_grad):
    full = out_grad.shape[1]
    width = full // 4
    me = (lax.axis_index("row") * 8 + lax.axis_index("col")) * 2 + lax.axis_index("rep")
    places = lax.dynamic_index_in_dim(jnp.asarray(tables()), me, 0, keepdims=False)
    tie = lax.optimization_barrier

    x1, z1 = send(out_grad, X_RING), send(out_grad, Z_RING)
    other = send(activations, REP_SWAP)
    up, down = send(activations, Y_RING), send(activations, Y_BACK)
    x1, z1, other, up, down = tie((x1, z1, other, up, down))

    x2, z2 = send(x1, X_RING), send(z1, Z_RING)
    far = send(up, Y_RING)
    other_up = send(other, Y_RING)
    swap_1 = send(join([activations, up, down]), CORE_SWAP)
    x3, z3 = send(x2, X_RING), send(z2, Z_RING)
    x2, z2, far, other, other_up, swap_1 = tie((x2, z2, far, other, other_up, swap_1))

    other_far, other_down = send(other_up, Y_RING), send(other, Y_BACK)
    swap_2 = [send(far, CORE_SWAP), send(join([other, other_up]), CORE_SWAP)]
    mine = whole([activations, up, down, far])
    left_own = sort_tokens(places, 0, mine + whole([swap_1, swap_2[0]]))
    left_own, x3, z3 = tie((left_own, x3, z3))
    first = [out_grad, x1, x2, z2]
    sums = [multiply([left_own, None], 0, first, [[], []], g, None, None, full) for g in range(2)]
    other_far, other_down, swap_2 = tie((other_far, other_down, swap_2))

    swap_3 = [send(join([other_down, other_far]), CORE_SWAP)]
    others = whole([other, other_up, other_down, other_far])
    left_other = sort_tokens(places, 1, others + whole([swap_2[1]] + swap_3))

    a, b = [[], []], [[], []]
    for g in range(2):
        at = 2 * g * width
        a[g].append(send(join([x1, x2, x3], slice(at, at + width)), Z_RING))
        b[g].append(send(join([z1, z2, z3], slice(at + width, at + 2 * width)), X_RING))
    a[0][0], b[0][0], sums[0] = tie((a[0][0], b[0][0], sums[0]))
    a[1][0], b[1][0], left_other, sums[1] = tie((a[1][0], b[1][0], left_other, sums[1]))
    lefts = [left_own, left_other]
    for g in range(2):
        sums[g] = multiply(lefts, 1, [x3, z1, z3], (a[g][:1], b[g][:1]), g, sums[g], None, full)
    for step in range(2):
        for g in range(2):
            if step == 1 and g == 0:
                a[g][1], b[g][1], sums[g] = tie((a[g][1], b[g][1], sums[g]))
            a[g].append(send(a[g][-1], Z_RING))
            b[g].append(send(b[g][-1], X_RING))
    result = None
    for g in range(2):
        result = multiply(lefts, 2, [], (a[g][1:], b[g][1:]), g, sums[g], result, full)
    return result


def solution(mesh):
    placed = (P(("col", "rep"), "row"), P(("row", "rep"), "col"))
    return jax.shard_map(
        shards, mesh=mesh, in_specs=placed, out_specs=P("row", "col"), check_vma=False
    )
```

```python
import jax
import jax.numpy as jnp
import numpy as np
from jax import lax
from jax.experimental import pallas as pl
from jax.experimental.pallas import tpu as pltpu
from jax.sharding import PartitionSpec as P

AXES = ("row", "col", "rep")
TOK = 128
LIMIT = 19
STEP = 512
F32 = jnp.float32
BF16 = jnp.bfloat16


def device(x, y, z, core):
    return ((z // 2) * 4 + x) * 16 + (y * 2 + core) * 2 + z % 2


def every():
    return [(x, y, z, c) for x in range(4) for y in range(4) for z in range(4) for c in range(2)]


def ring(dx, dy, dz):
    pairs = []
    for x, y, z, c in every():
        s = 1 if c == 0 else -1
        to = ((x + s * dx) % 4, (y + s * dy) % 4, (z + s * dz) % 4, c)
        pairs.append((device(x, y, z, c), device(*to)))
    return pairs


X_RING, Z_RING = ring(1, 0, 0), ring(0, 0, 1)
Y_RING, Y_BACK = ring(0, 1, 0), ring(0, -1, 0)
CORE_SWAP = [(device(x, y, z, c), device(x, y, z, 1 - c)) for x, y, z, c in every()]
REP_SWAP = [(device(x, y, z, c), device(x, y, z ^ 1, c)) for x, y, z, c in every()]

KINDS = [
    [(0, 0), (1, 0), (2, 0), (0, 2), (3, 0), (1, 2), (2, 2), (3, 2)],
    [(i, j) for j in (1, 3) for i in range(4)],
]


def inner(part, step):
    return [(i, step) if part == 0 else (step, i) for i in (1, 2, 3)]


PASSES = [
    [[(0, 0), (1, 0), (2, 0), (0, 2)] for p in range(2)],
    [[(3, 0), (0, 1), (0, 3)] + inner(p, 1) for p in range(2)],
    [inner(p, 2) + inner(p, 3) for p in range(2)],
]


def tables():
    out = np.zeros((128, 2, 8), np.int32)
    for x0, y0, z0, c0 in every():
        s0 = 1 if c0 == 0 else -1
        for kind in range(2):
            for at, (i, j) in enumerate(KINDS[kind]):
                x, z = (x0 - s0 * i) % 4, (z0 - s0 * j) % 4
                assert z % 2 == (z0 + kind) % 2
                k = (z // 2) * 4 + x
                y, c = k // 2, k % 2
                s = 1 if c == 0 else -1
                back = ((y0 - y) * s) % 4
                out[device(x0, y0, z0, c0), kind, int(c != c0) * 4 + (0, 1, 3, 2)[back]] = at
    return out


def sort_tokens(places, kind, pieces):
    arrays = [p[0] for p in pieces]
    wide = arrays[0].shape[1]

    def kernel(places_ref, *refs):
        sems = refs[-1]
        copies = []
        for ref, (_, first, blocks) in zip(refs, pieces):
            for b in range(blocks):
                n = len(copies)
                to = pl.multiple_of(places_ref[kind, n] * TOK, TOK)
                copies.append(
                    pltpu.make_async_copy(
                        ref.at[pl.ds(first + b * TOK, TOK)], refs[-2].at[pl.ds(to, TOK)], sems.at[n]
                    )
                )
                copies[-1].start()
        for copy in copies:
            copy.wait()

    total = TOK * 8
    return pl.pallas_call(
        kernel,
        grid_spec=pltpu.PrefetchScalarGridSpec(
            num_scalar_prefetch=1,
            grid=(1,),
            in_specs=[pl.BlockSpec(memory_space=pl.ANY) for a in arrays],
            out_specs=pl.BlockSpec(memory_space=pl.ANY),
            scratch_shapes=[pltpu.SemaphoreType.DMA((8,))],
        ),
        out_shape=jax.ShapeDtypeStruct((total, wide), BF16),
        compiler_params=pltpu.CompilerParams(vmem_limit_bytes=1 << 20),
        cost_estimate=pl.CostEstimate(flops=0, bytes_accessed=4 * wide * total, transcendentals=0),
    )(places, *arrays)


def multiply(lefts, number, shared, own, group, partial, before, full):
    width = full // 4
    used = [l for l in lefts if l is not None]
    slot = [None if l is None else sum(m is not None for m in lefts[:n]) for n, l in enumerate(lefts)]
    rows = used[0].shape[1]
    step = STEP
    order = PASSES[number]
    depth = TOK * len(order[0])
    n_own = len(own[0])
    skip = (4 if number in (1, 2) else 0, 0)

    def kernel(*refs):
        left_refs, refs = refs[: len(used)], refs[len(used) :]
        shared_refs, refs = refs[: len(shared)], refs[len(shared) :]
        own_refs = [refs[:n_own], refs[n_own : 2 * n_own]]
        refs = refs[2 * n_own :]
        out_ref = refs[-1]
        for part in range(2):
            cols = slice(part * width, (part + 1) * width)
            lhs = []
            for i, j in order[part]:
                at = (KINDS[j % 2].index((i, j)) - skip[j % 2]) * TOK
                lhs.append(left_refs[slot[j % 2]][at : at + TOK, :])
            lhs = jnp.concatenate(lhs, axis=0)
            rhs = [r[:, cols] for r in shared_refs] + [r[...] for r in own_refs[part]]
            rhs = jnp.concatenate(rhs, axis=0)
            total = lax.dot_general(lhs, rhs, (((0,), (0,)), ((), ())), preferred_element_type=F32)
            if partial is not None:
                total = total + refs[0][:, cols]
            out_ref[:, cols] = total.astype(out_ref.dtype)

    once = pl.Buffered(1)
    operands = used + list(shared) + list(own[0]) + list(own[1])
    in_specs = [pl.BlockSpec((4 * TOK, step), lambda m: (skip[0] // 4, m))]
    in_specs += [pl.BlockSpec((8 * TOK, step), lambda m: (0, m)) for _ in used[1:]]
    in_specs += [pl.BlockSpec((TOK, 2 * width), lambda m: (0, group), pipeline_mode=once) for _ in shared]
    in_specs += [pl.BlockSpec(b.shape, lambda m: (0, 0), pipeline_mode=once) for b in own[0] + own[1]]
    aliases = {}
    if partial is not None:
        if number < 2:
            aliases = {len(operands): 0}
        operands.append(partial)
        in_specs.append(pl.BlockSpec((step, 2 * width), lambda m: (m, 0)))
    if number == 2:
        out_specs = pl.BlockSpec((step, 2 * width), lambda m: (m, group))
        out_shape = jax.ShapeDtypeStruct((rows, full), BF16)
        if before is not None:
            aliases = {len(operands): 0}
            operands.append(before)
            in_specs.append(pl.BlockSpec(memory_space=pl.ANY))
    else:
        out_specs = pl.BlockSpec((step, 2 * width), lambda m: (m, 0))
        out_shape = jax.ShapeDtypeStruct((rows, 2 * width), F32)
    return pl.pallas_call(
        kernel,
        grid=(rows // step,),
        in_specs=in_specs,
        out_specs=out_specs,
        out_shape=out_shape,
        input_output_aliases=aliases,
        compiler_params=pltpu.CompilerParams(vmem_limit_bytes=LIMIT << 20),
        cost_estimate=pl.CostEstimate(
            flops=4 * rows * width * depth,
            bytes_accessed=4 * rows * TOK * 8 + 4 * depth * width + 12 * rows * width,
            transcendentals=0,
        ),
    )(*operands)


def send(block, pairs):
    return lax.ppermute(block, AXES, pairs)


def join(blocks, cols=slice(None)):
    return jnp.concatenate([b[:, cols] for b in blocks], axis=0)


def whole(arrays):
    return [(a, 0, a.shape[0] // TOK) for a in arrays]


def shards(activations, out_grad):
    full = out_grad.shape[1]
    width = full // 4
    me = (lax.axis_index("row") * 8 + lax.axis_index("col")) * 2 + lax.axis_index("rep")
    places = lax.dynamic_index_in_dim(jnp.asarray(tables()), me, 0, keepdims=False)
    tie = lax.optimization_barrier

    x1, z1 = send(out_grad, X_RING), send(out_grad, Z_RING)
    other = send(activations, REP_SWAP)
    up, down = send(activations, Y_RING), send(activations, Y_BACK)
    x1, z1, other, up, down, places = tie((x1, z1, other, up, down, places))

    x2, z2 = send(x1, X_RING), send(z1, Z_RING)
    far = send(up, Y_RING)
    other_up = send(other, Y_RING)
    swap_1 = send(join([activations, up, down]), CORE_SWAP)
    x3, z3 = send(x2, X_RING), send(z2, Z_RING)
    x2, z2, far, other, other_up, swap_1 = tie((x2, z2, far, other, other_up, swap_1))

    other_far, other_down = send(other_up, Y_RING), send(other, Y_BACK)
    swap_2 = [send(far, CORE_SWAP), send(join([other, other_up]), CORE_SWAP)]
    mine = whole([activations, up, down, far])
    left_own = sort_tokens(places, 0, mine + whole([swap_1, swap_2[0]]))
    left_own, x3, z3 = tie((left_own, x3, z3))
    first = [out_grad, x1, x2, z2]
    sums = [multiply([left_own, None], 0, first, [[], []], g, None, None, full) for g in range(2)]
    other_far, other_down, swap_2 = tie((other_far, other_down, swap_2))

    swap_3 = [send(join([other_down, other_far]), CORE_SWAP)]
    others = whole([other, other_up, other_down, other_far])
    left_other = sort_tokens(places, 1, others + whole([swap_2[1]] + swap_3))

    a, b = [[], []], [[], []]
    for g in range(2):
        at = 2 * g * width
        a[g].append(send(join([x1, x2, x3], slice(at, at + width)), Z_RING))
        b[g].append(send(join([z1, z2, z3], slice(at + width, at + 2 * width)), X_RING))
    a[0][0], b[0][0], sums[0] = tie((a[0][0], b[0][0], sums[0]))
    a[1][0], b[1][0], left_other, sums[1] = tie((a[1][0], b[1][0], left_other, sums[1]))
    lefts = [left_own, left_other]
    for g in range(2):
        sums[g] = multiply(lefts, 1, [x3, z1, z3], (a[g][:1], b[g][:1]), g, sums[g], None, full)
    for step in range(2):
        for g in range(2):
            if step == 1 and g == 0:
                a[g][1], b[g][1], sums[g] = tie((a[g][1], b[g][1], sums[g]))
            a[g].append(send(a[g][-1], Z_RING))
            b[g].append(send(b[g][-1], X_RING))
    result = None
    for g in range(2):
        result = multiply(lefts, 2, [], (a[g][1:], b[g][1:]), g, sums[g], result, full)
    return result


def solution(mesh):
    placed = (P(("col", "rep"), "row"), P(("row", "rep"), "col"))
    return jax.shard_map(
        shards, mesh=mesh, in_specs=placed, out_specs=P("row", "col"), check_vma=False
    )
```
